32 devices in a mesh: row: 4 (over y, x), col: 8 (over z, core).
Axes of the slice: x: 2, y: 2, z: 4, core: 2. Of those that a mesh axis runs over, the one named last changes fastest.
Arguments:
- data: bfloat16 [4, 8, 32, 1024, 128], P('row', 'col'), may hold values from -6 to 6
- real_index: int32 [4, 8, 2, 2], P('row', 'col'), may hold values from 0 to 31
- latent_seed: int32 [4, 8, 2, 2], P('row', 'col'), may hold values from 0 to 255
- latent_bank: float32 [256, 128], replicated, may hold values from -6 to 6
- g_in: float32 [4, 8, 128, 128], P('row', 'col'), may hold values from -0.5 to 0.5
- g_base: float32 [4, 8, 1024, 128], P('row', 'col'), may hold values from -6 to 6
- g_one: float32 [4, 8, 128, 128], P('row', 'col'), may hold values from -0.5 to 0.5
- g_two: float32 [4, 8, 128, 128], P('row', 'col'), may hold values from -0.5 to 0.5
- d_one: float32 [4, 8, 128, 128], P('row', 'col'), may hold values from -0.5 to 0.5
- d_two: float32 [4, 8, 128, 128], P('row', 'col'), may hold values from -0.5 to 0.5
- d_out: float32 [4, 8, 128], P('row', 'col'), may hold values from -0.5 to 0.5
Outputs:
- new_g_in: float32 [4, 8, 128, 128], P('row', 'col')
- new_g_base: float32 [4, 8, 1024, 128], P('row', 'col')
- new_g_one: float32 [4, 8, 128, 128], P('row', 'col')
- new_g_two: float32 [4, 8, 128, 128], P('row', 'col')
- new_d_one: float32 [4, 8, 128, 128], P('row', 'col')
- new_d_two: float32 [4, 8, 128, 128], P('row', 'col')
- new_d_out: float32 [4, 8, 128], P('row', 'col')
- verdicts: float32 [4, 8, 2, 12], P('row', 'col')
The draws below stay inside these ranges and needn't reach their ends.
All inputs are finite; a program needn't handle non-finite values.
Results may differ from the reference program's by a relative error of at most 0.0028.
Values may be sent and summed in bfloat16 or wider, within the bound.
A program may use at most 128 MiB of HBM per device.

```python
import jax
import jax.numpy as jnp
from jax import lax

POSITIONS = 1024
CHANNELS = 128
LATENT = 128
FAKES = 2
REALS = 2
DATA = 32
BANK = 256
STEPS = 2
GRID_ROWS = 4
GRID_COLS = 8


def set_ends(array, rng, low, high):
    dims = array.shape
    spot = [jax.random.randint(jax.random.fold_in(rng, axis), (), 0, dims[axis]) for axis in range(len(dims))]
    array = array.at[tuple(spot)].set(low)
    longest = dims.index(max(dims))
    spot[longest] = (spot[longest] + 1) % dims[longest]
    return array.at[tuple(spot)].set(high)


def level_of(stream_key, shape, cuts, low, top_value):
    factor_of = 1.0
    for position, shards_of in cuts:
        steps = jax.random.uniform(jax.random.fold_in(jax.random.fold_in(stream_key, 6), position), (shards_of,), jnp.float32, low / len(cuts), top_value / len(cuts))
        factor_of = factor_of * jnp.repeat(jnp.exp(steps), shape[position] // shards_of).reshape((-1,) + (1,) * (len(shape) - 1 - position))
    return factor_of


def scatter_about(stream_key, extent, deviation, most, split=(), kind=jnp.bfloat16):
    factor_of = level_of(stream_key, extent, split, -0.22, 0.18) if split else 1.0
    values = jax.random.normal(stream_key, extent, jnp.float32) * deviation * factor_of
    return jnp.minimum(jnp.maximum(values, -most), most).astype(kind)


def setup_inputs(seed: int = 0) -> dict:
    streams_of = jax.random.split(jax.random.key(seed), 12)
    return {
        "data": scatter_about(streams_of[0], (GRID_ROWS, GRID_COLS, DATA, POSITIONS, CHANNELS), 1.0, 6.0, ((0, 4), (1, 8))),
        "real_index": set_ends(jax.random.randint(streams_of[1], (GRID_ROWS, GRID_COLS, STEPS, REALS), 0, DATA), jax.random.fold_in(streams_of[1], 1), 0, DATA - 1).astype(jnp.int32),
        "latent_seed": set_ends(jax.random.randint(streams_of[2], (GRID_ROWS, GRID_COLS, STEPS, FAKES), 0, BANK), jax.random.fold_in(streams_of[2], 1), 0, BANK - 1).astype(jnp.int32),
        "latent_bank": scatter_about(streams_of[3], (BANK, LATENT), 1.0, 6.0, (), jnp.float32),
        "g_in": scatter_about(streams_of[4], (GRID_ROWS, GRID_COLS, LATENT, CHANNELS), LATENT ** -0.5, 0.5, ((0, 4), (1, 8)), jnp.float32),
        "g_base": scatter_about(streams_of[5], (GRID_ROWS, GRID_COLS, POSITIONS, CHANNELS), 1.0, 6.0, ((0, 4), (1, 8)), jnp.float32),
        "g_one": scatter_about(streams_of[6], (GRID_ROWS, GRID_COLS, CHANNELS, CHANNELS), CHANNELS ** -0.5, 0.5, ((0, 4), (1, 8)), jnp.float32),
        "g_two": scatter_about(streams_of[7], (GRID_ROWS, GRID_COLS, CHANNELS, CHANNELS), CHANNELS ** -0.5, 0.5, ((0, 4), (1, 8)), jnp.float32),
        "d_one": scatter_about(streams_of[8], (GRID_ROWS, GRID_COLS, CHANNELS, CHANNELS), CHANNELS ** -0.5, 0.5, ((0, 4), (1, 8)), jnp.float32),
        "d_two": scatter_about(streams_of[9], (GRID_ROWS, GRID_COLS, CHANNELS, CHANNELS), CHANNELS ** -0.5, 0.5, ((0, 4), (1, 8)), jnp.float32),
        "d_out": scatter_about(streams_of[10], (GRID_ROWS, GRID_COLS, CHANNELS), CHANNELS ** -0.5, 0.5, ((0, 4), (1, 8)), jnp.float32),
    }


learn_rate = 0.05
base_rate = 0.1


def matmul(left_side, right_side):
    return jnp.dot(left_side.astype(jnp.float32), right_side.astype(jnp.float32), preferred_element_type=jnp.float32)


def rows_matmul(left_side, right_side):
    return lax.dot_general(left_side.astype(jnp.float32), right_side.astype(jnp.float32), (((0,), (0,)), ((), ())), preferred_element_type=jnp.float32)


def silu_slope(values):
    sigmoid_part = jax.nn.sigmoid(values)
    return sigmoid_part * (1.0 + values * (1.0 - sigmoid_part))


def generate(latent, weights):
    w_in, w_base, w_one, w_two = weights
    shifted = matmul(latent, w_in)
    batch_count = latent.shape[0]
    places, channels = w_base.shape
    gen_pre = (w_base.astype(jnp.float32)[None] + shifted[:, None, :]).reshape(batch_count * places, channels)
    hidden = jax.nn.silu(gen_pre).astype(jnp.bfloat16)
    middle_pre = matmul(hidden, w_one)
    middle = jax.nn.silu(middle_pre).astype(jnp.bfloat16)
    own_fakes = (lax.optimization_barrier(hidden).astype(jnp.float32) + matmul(middle, w_two)).astype(jnp.bfloat16)
    return own_fakes, (gen_pre, hidden, middle_pre, middle)


def generator_grads(cotangent, stored, latent, weights):
    gen_pre, hidden, middle_pre, middle = stored
    w_in, w_base, w_one, w_two = weights
    repeats = cotangent.shape[0] // hidden.shape[0]
    grad_two = rows_matmul(jnp.tile(middle, (repeats, 1)), cotangent)
    inner_term = matmul(cotangent, w_two.T) * jnp.tile(silu_slope(middle_pre), (repeats, 1))
    inner_half = inner_term.astype(jnp.bfloat16)
    grad_one = rows_matmul(jnp.tile(hidden, (repeats, 1)), inner_half)
    outer_term = (cotangent.astype(jnp.float32) + matmul(inner_half, w_one.T)) * jnp.tile(silu_slope(gen_pre), (repeats, 1))
    batch_count = latent.shape[0]
    places, channels = w_base.shape
    outer_term = outer_term.reshape(repeats, batch_count, places, channels)
    grad_base = jnp.sum(outer_term, axis=(0, 1))
    grad_in = jnp.dot(latent.astype(jnp.float32).T, jnp.sum(outer_term, axis=(0, 2)), precision=lax.Precision.HIGHEST)
    return grad_in, grad_base, grad_one, grad_two


def judge(images, d_one, d_two, d_out, batch_count):
    places = images.shape[0] // batch_count
    first_pre = matmul(images, d_one)
    first_act = jax.nn.silu(first_pre).astype(jnp.bfloat16)
    summed = images.astype(jnp.float32) + matmul(first_act, d_two)
    feature = jax.nn.silu(summed)
    verdict = jnp.sum(feature * d_out[None, :], axis=1).reshape(batch_count, places).mean(axis=1)
    return verdict, (first_pre, first_act, summed, feature)


def judge_back(slopes, stored, d_two, d_out, places):
    first_pre, first_act, summed, feature = stored
    weight_rows = jnp.repeat(slopes / places, places)
    outer_term = weight_rows[:, None] * d_out[None, :] * silu_slope(summed)
    outer_half = outer_term.astype(jnp.bfloat16)
    inner_half = (matmul(outer_half, d_two.T) * silu_slope(first_pre)).astype(jnp.bfloat16)
    return weight_rows, outer_term, outer_half, inner_half


def judge_cell_math(images, d_half, d_out, batch_count, fake_count, places):
    d_one, d_two = d_half
    verdict, stored = judge(images, d_one, d_two, d_out, batch_count)
    fake_verdict = verdict[:fake_count]
    real_verdict = verdict[fake_count:]
    disc_slope = jnp.concatenate([jax.nn.sigmoid(fake_verdict), -jax.nn.sigmoid(-real_verdict)])
    weight_rows, outer_term, outer_half, inner_half = judge_back(disc_slope, stored, d_two, d_out, places)
    grad_out = jnp.sum(stored[3] * weight_rows[:, None], axis=0)
    grad_two = rows_matmul(stored[1], outer_half)
    grad_one = rows_matmul(images, inner_half)
    fake_rows = fake_count * places
    fake_stored = tuple(member[:fake_rows] for member in stored)
    gen_slope = -jax.nn.sigmoid(-fake_verdict)
    unused, gen_outer, gen_half, gen_inner = judge_back(gen_slope, fake_stored, d_two, d_out, places)
    returned = (gen_outer + matmul(gen_inner, d_one.T)).astype(jnp.bfloat16)
    return verdict, (grad_one, grad_two, grad_out), returned


def reference(data, real_index, latent_seed, latent_bank, g_in, g_base, g_one, g_two, d_one, d_two, d_out):
    grid_rows = data.shape[0]
    grid_cols = data.shape[1]
    cells = grid_rows * grid_cols
    places = data.shape[3]
    channels = data.shape[4]
    batch_count = latent_seed.shape[3]
    reals_count = real_index.shape[3]
    fake_count = 5 * batch_count
    step_sizes = [learn_rate, base_rate * places, learn_rate, learn_rate, learn_rate, learn_rate, learn_rate]
    data_flat = data.reshape((cells,) + data.shape[2:])
    real_flat = real_index.reshape(cells, STEPS, reals_count)
    seed_flat = latent_seed.reshape(cells, STEPS, batch_count)
    params = [member.reshape((cells,) + member.shape[2:]) for member in (g_in, g_base, g_one, g_two, d_one, d_two, d_out)]
    bank_half = latent_bank.astype(jnp.bfloat16)
    cell_ids = jnp.arange(cells).astype(jnp.int32)
    rows_of = cell_ids // grid_cols
    cols_of = cell_ids % grid_cols
    north = ((rows_of - 1) % grid_rows) * grid_cols + cols_of
    south = ((rows_of + 1) % grid_rows) * grid_cols + cols_of
    west = rows_of * grid_cols + (cols_of - 1) % grid_cols
    east = rows_of * grid_cols + (cols_of + 1) % grid_cols
    neighbour_ids = jnp.stack([cell_ids, north, south, west, east], axis=1).astype(jnp.int32)
    verdict_list = []
    for step_index in range(STEPS):
        latents = bank_half[seed_flat[:, step_index]]
        halves = [member.astype(jnp.bfloat16) for member in params[:6]]

        def make_fakes(cell):
            return generate(latents[cell], tuple(member[cell] for member in halves[:4]))[0]

        all_fakes = lax.map(make_fakes, cell_ids)

        def judge_cell(cell):
            chosen = neighbour_ids[cell]
            judged = all_fakes[chosen].reshape(fake_count * places, channels)
            real_rows = data_flat[cell][real_flat[cell, step_index]].reshape(reals_count * places, channels)
            images = jnp.concatenate([judged, real_rows], axis=0)
            verdict, grads, returned = judge_cell_math(images, (halves[4][cell], halves[5][cell]), params[6][cell], fake_count + reals_count, fake_count, places)
            return verdict, grads, returned.reshape(5, batch_count * places, channels)

        verdict_all, disc_grads, returned_all = lax.map(judge_cell, cell_ids)

        def gen_cell(cell):
            chosen = neighbour_ids[cell]
            incoming = jnp.concatenate([returned_all[cell, 0], returned_all[chosen[1], 2], returned_all[chosen[2], 1], returned_all[chosen[3], 4], returned_all[chosen[4], 3]], axis=0)
            weights = tuple(member[cell] for member in halves[:4])
            own_fakes, stored = generate(latents[cell], weights)
            return generator_grads(incoming, stored, latents[cell], weights)

        gen_grads = lax.map(gen_cell, cell_ids)
        all_grads = list(gen_grads) + list(disc_grads)
        params = [member - step_size * grad for member, grad, step_size in zip(params, all_grads, step_sizes)]
        verdict_list.append(verdict_all)
    verdicts = jnp.stack(verdict_list, axis=1).reshape(grid_rows, grid_cols, STEPS, fake_count + reals_count)
    finals = [member.reshape((grid_rows, grid_cols) + member.shape[1:]) for member in params]
    return finals[0], finals[1], finals[2], finals[3], finals[4], finals[5], finals[6], verdicts
```

```python
import functools

import jax
import jax.numpy as jnp
from jax import lax
from jax.experimental import pallas as pl
from jax.experimental.pallas import tpu as pltpu
from jax.sharding import PartitionSpec as P

learn_rate = 0.05
base_rate = 0.1

TILE = 256
MESH = pl.DeviceIdType.MESH
f32 = jnp.float32
bf16 = jnp.bfloat16


def dot(left, right):
    return jnp.dot(left, right, preferred_element_type=f32)


def rows_dot(left, right):
    return lax.dot_general(left, right, (((0,), (0,)), ((), ())), preferred_element_type=f32)


def sigmoid(values):
    return 0.5 + 0.5 * jnp.tanh(0.5 * values)


def silu_parts(values):
    gate = sigmoid(values)
    act = values * gate
    return act, gate + act * (1.0 - gate)


def pair_lanes(left, right):
    return jnp.concatenate([left, right], axis=1)


def put_blocks(ref, weights):
    size = weights.shape[0]
    nothing = jnp.zeros((size, size), bf16)
    ref[...] = jnp.concatenate(
        [pair_lanes(weights, nothing), pair_lanes(nothing, weights)], axis=0
    )


def half_sum(blocks, scale):
    size = blocks.shape[0] // 2
    return (
        blocks[:size, :size] * scale[:, :size] + blocks[size:, size:] * scale[:, size:]
    )


def opposite(way):
    return way + 1 - 2 * lax.rem(way, 2)


def train_kernel(
    rows_count,
    cols_count,
    steps,
    reals_ref, seed_ref, bank_ref,
    g_in_ref, g_base_ref, g_one_ref, g_two_ref, d_one_ref, d_two_ref, d_out_ref,
    n_in, n_base, n_one, n_two, n_done, n_dtwo, n_dout, verdict_ref,
    small_own, base_own, small_in, base_in,
    cot_own, cot_out, cot_in, scale_own, scale_out, scale_in,
    hidden_s, middle_s, slope_pre_s, slope_mid_s,
    one_b, two_b, one_tb, two_tb, own_one_tb, own_two_tb,
    d1_b, d2_b, d1_tb, d2_tb,
    acc_one, acc_two, acc_feat, sum_done, sum_dtwo, sum_dout,
    latent_s,
    fwd_send, fwd_recv, ret_send, ret_recv, sc_send, sc_recv,
):
    places, channels = g_base_ref.shape
    tiles = places // TILE
    my_row = lax.axis_index("row")
    my_col = lax.axis_index("col")

    def device_of(way):
        along = 2 * lax.rem(way, 2) - 1
        vertical = 1 - way // 2
        row = lax.rem(my_row + along * vertical + rows_count, rows_count)
        col = lax.rem(my_col + along * (1 - vertical) + cols_count, cols_count)
        return (row, col)

    def rows_of(tile):
        return pl.ds(pl.multiple_of(tile * TILE, TILE), TILE)

    def small_copy(step, way, slot):
        return pltpu.make_async_remote_copy(
            src_ref=small_own, dst_ref=small_in.at[step, slot],
            send_sem=fwd_send.at[step, way, 0], recv_sem=fwd_recv.at[step, slot, 0],
            device_id=device_of(way), device_id_type=MESH,
        )

    def base_copy(step, way, slot, tile):
        return pltpu.make_async_remote_copy(
            src_ref=base_own.at[rows_of(tile)], dst_ref=base_in.at[step, slot, rows_of(tile)],
            send_sem=fwd_send.at[step, way, tile + 1], recv_sem=fwd_recv.at[step, slot, tile + 1],
            device_id=device_of(way), device_id_type=MESH,
        )

    def cot_copy(step, way, slot, tile):
        return pltpu.make_async_remote_copy(
            src_ref=cot_out.at[step, way, rows_of(tile)],
            dst_ref=cot_in.at[step, slot, rows_of(tile)],
            send_sem=ret_send.at[step, way, tile], recv_sem=ret_recv.at[step, slot, tile],
            device_id=device_of(way), device_id_type=MESH,
        )

    def scale_copy(step, way, slot):
        return pltpu.make_async_remote_copy(
            src_ref=scale_out.at[step, way], dst_ref=scale_in.at[step, slot],
            send_sem=sc_send.at[step, way], recv_sem=sc_recv.at[step, slot],
            device_id=device_of(way), device_id_type=MESH,
        )

    barrier = pltpu.get_barrier_semaphore()
    for way in range(4):
        pl.semaphore_signal(barrier, inc=1, device_id=device_of(way), device_id_type=MESH)

    n_in[...] = g_in_ref[...]
    n_base[...] = g_base_ref[...]
    n_one[...] = g_one_ref[...]
    n_two[...] = g_two_ref[...]
    n_done[...] = d_one_ref[...]
    n_dtwo[...] = d_two_ref[...]
    n_dout[...] = d_out_ref[...]
    bank_rows = bank_ref.shape[0]
    chosen = seed_ref[...] == lax.broadcasted_iota(jnp.int32, (seed_ref.shape[0], bank_rows), 1)
    latent_s[...] = dot(chosen.astype(f32).astype(bf16), bank_ref[...].astype(bf16)).reshape(
        latent_s.shape
    )
    verdict_ref[...] = jnp.zeros_like(verdict_ref)
    pl.semaphore_wait(barrier, 4)

    def shifts_of(small):
        hi = small[2 * channels : 2 * channels + 16].astype(f32)
        return hi[0:1] + hi[2:3] + hi[4:5], hi[1:2] + hi[3:4] + hi[5:6]

    def made(base, shift_a, shift_b, one, two, keep):
        base = base.astype(f32)
        gen_pre = pair_lanes(base + shift_a, base + shift_b)
        act, slope = silu_parts(gen_pre)
        hidden = act.astype(bf16)
        middle_pre = dot(hidden, one)
        act_mid, slope_mid = silu_parts(middle_pre)
        middle = act_mid.astype(bf16)
        if keep is not None:
            hidden_s[keep] = hidden
            middle_s[keep] = middle
            slope_pre_s[keep] = slope
            slope_mid_s[keep] = slope_mid
        return (hidden.astype(f32) + dot(middle, two)).astype(bf16)

    def judge_tile(images, d_out_pair):
        first_pre = dot(images, d1_b[...])
        act, slope_first = silu_parts(first_pre)
        first = act.astype(bf16)
        summed = images.astype(f32) + dot(first, d2_b[...])
        feature, slope_sum = silu_parts(summed)
        acc_feat[...] += jnp.sum(feature, axis=0, keepdims=True)
        outer = slope_sum * d_out_pair
        outer_half = outer.astype(bf16)
        inner = (dot(outer_half, d2_tb[...]) * slope_first).astype(bf16)
        acc_two[...] += rows_dot(first, outer_half)
        acc_one[...] += rows_dot(images, inner)
        return outer, inner

    def clear():
        acc_feat[...] = jnp.zeros_like(acc_feat)
        acc_one[...] = jnp.zeros_like(acc_one)
        acc_two[...] = jnp.zeros_like(acc_two)

    def settle(step, place, real):
        feats = acc_feat[...]
        weighted = feats * pair_lanes(n_dout[...], n_dout[...])
        shape = (1, channels)
        low = jnp.sum(weighted[:, :channels], axis=1, keepdims=True) * (1.0 / places)
        high = jnp.sum(weighted[:, channels:], axis=1, keepdims=True) * (1.0 / places)
        low = jnp.broadcast_to(low, shape)
        high = jnp.broadcast_to(high, shape)
        verdict_ref[step, place] = jnp.concatenate(
            [low, high, jnp.zeros((6, channels), f32)], axis=0
        )
        verdict = pair_lanes(low, high)
        against = -sigmoid(-verdict) * (1.0 / places)
        toward = against if real else sigmoid(verdict) * (1.0 / places)
        sum_done[...] += half_sum(acc_one[...], toward)
        sum_dtwo[...] += half_sum(acc_two[...], toward)
        scaled = feats * toward
        sum_dout[...] += scaled[:, :channels] + scaled[:, channels:]
        return jnp.broadcast_to(against, (8, 2 * channels))

    def one_step(step, carry):
        base_own[...] = n_base[...].astype(bf16)
        latent = latent_s[step].astype(bf16)
        shift = dot(latent, n_in[...].astype(bf16))
        top = shift.astype(bf16)
        rest = shift - top.astype(f32)
        mid = rest.astype(bf16)
        last = rest - mid.astype(f32)
        small_own[0:channels] = n_one[...].astype(bf16)
        small_own[channels : 2 * channels] = n_two[...].astype(bf16)
        small_own[2 * channels : 2 * channels + 16] = jnp.concatenate(
            [top[0:2].astype(f32), mid[0:2].astype(f32), last[0:2], jnp.zeros((10, channels), f32)],
            axis=0,
        ).astype(bf16)

        def send_ways(way, carry):
            small_copy(step, way, opposite(way)).start()
            return carry

        def send_bases(at, carry):
            way = lax.rem(at, 4)
            base_copy(step, way, opposite(way), at // 4).start()
            return carry

        lax.fori_loop(0, 4, send_ways, 0)
        lax.fori_loop(0, 4 * tiles, send_bases, 0)

        put_blocks(one_b, n_one[...].astype(bf16))
        put_blocks(two_b, n_two[...].astype(bf16))
        put_blocks(own_one_tb, n_one[...].T.astype(bf16))
        put_blocks(own_two_tb, n_two[...].T.astype(bf16))
        put_blocks(d1_b, n_done[...].astype(bf16))
        put_blocks(d2_b, n_dtwo[...].astype(bf16))
        put_blocks(d1_tb, n_done[...].T.astype(bf16))
        put_blocks(d2_tb, n_dtwo[...].T.astype(bf16))
        sum_done[...] = jnp.zeros_like(sum_done)
        sum_dtwo[...] = jnp.zeros_like(sum_dtwo)
        sum_dout[...] = jnp.zeros_like(sum_dout)
        d_out_pair = pair_lanes(n_dout[...], n_dout[...])

        clear()

        def own_tile(tile, carry):
            at = rows_of(tile)
            images = made(base_own[at], shift[0:1], shift[1:2], one_b[...], two_b[...], at)
            outer, inner = judge_tile(images, d_out_pair)
            cot_own[at] = (outer + dot(inner, d1_tb[...])).astype(bf16)
            return carry

        lax.fori_loop(0, tiles, own_tile, 0)
        scale_own[...] = settle(step, 0, False)

        clear()

        def real_tile(tile, carry):
            at = rows_of(tile)
            judge_tile(pair_lanes(reals_ref[2 * step, at], reals_ref[2 * step + 1, at]), d_out_pair)
            return carry

        lax.fori_loop(0, tiles, real_tile, 0)
        settle(step, 5, True)

        def beside(order, carry):
            way = 3 - order
            small_copy(step, way, way).wait_recv()
            small = small_in.at[step, way]
            put_blocks(one_b, small[0:channels])
            put_blocks(two_b, small[channels : 2 * channels])
            shift_a, shift_b = shifts_of(small)
            clear()

            def their_tile(tile, carry):
                at = rows_of(tile)
                base_copy(step, way, way, tile).wait_recv()
                images = made(base_in[step, way, at], shift_a, shift_b, one_b[...], two_b[...], None)
                outer, inner = judge_tile(images, d_out_pair)
                cot_out[step, way, at] = (outer + dot(inner, d1_tb[...])).astype(bf16)
                cot_copy(step, way, opposite(way), tile).start()
                return carry

            lax.fori_loop(0, tiles, their_tile, 0)
            scale_out[step, way] = settle(step, way + 1, False)
            scale_copy(step, way, opposite(way)).start()
            return carry

        lax.fori_loop(0, 4, beside, 0)

        n_done[...] -= learn_rate * sum_done[...]
        n_dtwo[...] -= learn_rate * sum_dtwo[...]
        n_dout[...] -= learn_rate * sum_dout[...]

        clear()

        def scale_waits(way, carry):
            scale_copy(step, way, way).wait_recv()
            return carry

        lax.fori_loop(0, 4, scale_waits, 0)

        def back_tile(tile, carry):
            at = rows_of(tile)

            def cot_waits(way, carry):
                cot_copy(step, way, way, tile).wait_recv()
                return carry

            lax.fori_loop(0, 4, cot_waits, 0)
            total = cot_own[at].astype(f32) * scale_own[0:1]
            for way in range(4):
                total += cot_in[step, way, at].astype(f32) * scale_in[step, way, 0:1]
            half = total.astype(bf16)
            acc_two[...] += rows_dot(middle_s[at], half)
            inner = (dot(half, own_two_tb[...]) * slope_mid_s[at]).astype(bf16)
            acc_one[...] += rows_dot(hidden_s[at], inner)
            outer = (total + dot(inner, own_one_tb[...])) * slope_pre_s[at]
            acc_feat[...] += jnp.sum(outer, axis=0, keepdims=True)
            n_base[at] -= (base_rate * places) * (outer[:, :channels] + outer[:, channels:])
            return carry

        lax.fori_loop(0, tiles, back_tile, 0)
        n_one[...] -= learn_rate * (
            acc_one[:channels, :channels] + acc_one[channels:, channels:]
        )
        n_two[...] -= learn_rate * (
            acc_two[:channels, :channels] + acc_two[channels:, channels:]
        )
        sums = acc_feat[...]
        sums = jnp.concatenate(
            [sums[:, :channels], sums[:, channels:], jnp.zeros((6, channels), f32)], axis=0
        )
        n_in[...] -= learn_rate * lax.dot_general(
            latent_s[step], sums, (((0,), (0,)), ((), ())),
            precision=lax.Precision.HIGHEST, preferred_element_type=f32,
        )

        def sent(way, carry):
            small_copy(step, way, way).wait_send()
            scale_copy(step, way, way).wait_send()

            def sent_tile(tile, carry):
                base_copy(step, way, way, tile).wait_send()
                cot_copy(step, way, way, tile).wait_send()
                return carry

            return lax.fori_loop(0, tiles, sent_tile, carry)

        lax.fori_loop(0, 4, sent, 0)
        return carry

    lax.fori_loop(0, steps, one_step, 0)


def pick_kernel(index_ref, data_ref, out_ref):
    out_ref[...] = data_ref[...]


def pick(data, index):
    count = index.shape[0]
    block = (1,) + data.shape[1:]
    return pl.pallas_call(
        pick_kernel,
        out_shape=jax.ShapeDtypeStruct((count,) + data.shape[1:], data.dtype),
        grid_spec=pltpu.PrefetchScalarGridSpec(
            num_scalar_prefetch=1,
            grid=(count,),
            in_specs=[pl.BlockSpec(block, lambda i, index_ref: (index_ref[i], 0, 0))],
            out_specs=pl.BlockSpec(block, lambda i, index_ref: (i, 0, 0)),
        ),
    )(index, data)


def on_device(
    rows_count, cols_count,
    data, real_index, latent_seed, latent_bank, g_in, g_base, g_one, g_two, d_one, d_two, d_out,
):
    steps = real_index.shape[2]
    places, channels = data.shape[3:]
    reals = pick(data[0, 0], real_index.reshape(-1))
    seed = latent_seed.reshape(steps, 2)
    seed = jnp.concatenate([seed, jnp.full((steps, 6), -1, jnp.int32)], axis=1).reshape(-1, 1)
    wide = 2 * channels
    square = (channels, channels)
    blocks = pltpu.VMEM((wide, wide), bf16)
    tiles = places // TILE
    vmem = pl.BlockSpec(memory_space=pltpu.VMEM)
    small = 2 * channels + 16
    shapes = [square, (places, channels), square, square, square, square, (1, channels)]
    outs = pl.pallas_call(
        functools.partial(train_kernel, rows_count, cols_count, steps),
        out_shape=[jax.ShapeDtypeStruct(shape, f32) for shape in shapes]
        + [jax.ShapeDtypeStruct((steps, 6, 8, channels), f32)],
        in_specs=[vmem] * 10,
        out_specs=[vmem] * 8,
        scratch_shapes=[
            pltpu.VMEM((small, channels), bf16),
            pltpu.VMEM((places, channels), bf16),
            pltpu.VMEM((steps, 4, small, channels), bf16),
            pltpu.VMEM((steps, 4, places, channels), bf16),
            pltpu.VMEM((places, wide), bf16),
            pltpu.VMEM((steps, 4, places, wide), bf16),
            pltpu.VMEM((steps, 4, places, wide), bf16),
            pltpu.VMEM((8, wide), f32),
            pltpu.VMEM((steps, 4, 8, wide), f32),
            pltpu.VMEM((steps, 4, 8, wide), f32),
            pltpu.VMEM((places, wide), bf16),
            pltpu.VMEM((places, wide), bf16),
            pltpu.VMEM((places, wide), f32),
            pltpu.VMEM((places, wide), f32),
        ]
        + [blocks] * 10
        + [
            pltpu.VMEM((wide, wide), f32),
            pltpu.VMEM((wide, wide), f32),
            pltpu.VMEM((1, wide), f32),
            pltpu.VMEM(square, f32),
            pltpu.VMEM(square, f32),
            pltpu.VMEM((1, channels), f32),
            pltpu.VMEM((steps, 8, channels), f32),
            pltpu.SemaphoreType.DMA((steps, 4, tiles + 1)),
            pltpu.SemaphoreType.DMA((steps, 4, tiles + 1)),
            pltpu.SemaphoreType.DMA((steps, 4, tiles)),
            pltpu.SemaphoreType.DMA((steps, 4, tiles)),
            pltpu.SemaphoreType.DMA((steps, 4)),
            pltpu.SemaphoreType.DMA((steps, 4)),
        ],
        compiler_params=pltpu.CompilerParams(
            collective_id=0, has_side_effects=True, vmem_limit_bytes=50 * 1024 * 1024
        ),
    )(
        reals, seed, latent_bank,
        g_in[0, 0], g_base[0, 0], g_one[0, 0], g_two[0, 0], d_one[0, 0], d_two[0, 0],
        d_out.reshape(1, channels),
    )
    verdicts = outs[7][:, :, :2, 0].reshape(1, 1, steps, 12)
    finals = [member[None, None] for member in outs[:6]] + [outs[6].reshape(1, 1, channels)]
    return (*finals, verdicts)


def solution(mesh):
    whole = P("row", "col", None, None)
    return jax.shard_map(
        functools.partial(on_device, mesh.shape["row"], mesh.shape["col"]),
        mesh=mesh,
        in_specs=(P("row", "col", None, None, None), whole, whole, P()) + (whole,) * 6
        + (P("row", "col", None),),
        out_specs=(whole,) * 6 + (P("row", "col", None), whole),
        check_vma=False,
    )
```

```python
import functools

import jax
import jax.numpy as jnp
from jax import lax
from jax.experimental import pallas as pl
from jax.experimental.pallas import tpu as pltpu
from jax.sharding import PartitionSpec as P

learn_rate = 0.05
base_rate = 0.1

TILE = 512
MESH = pl.DeviceIdType.MESH
f32 = jnp.float32
bf16 = jnp.bfloat16


def dot(left, right):
    return jnp.dot(left, right, preferred_element_type=f32)


def rows_dot(left, right):
    return lax.dot_general(left, right, (((0,), (0,)), ((), ())), preferred_element_type=f32)


def sigmoid(values):
    return 0.5 + 0.5 * jnp.tanh(0.5 * values)


def silu_parts(values):
    half = 0.5 * values
    twice = 1.0 + jnp.tanh(half)
    act = half * twice
    return act, twice * ((1.0 + values) - act)


def pair_lanes(left, right):
    return jnp.concatenate([left, right], axis=1)


def put_blocks(ref, weights):
    size = weights.shape[0]
    nothing = jnp.zeros((size, size), bf16)
    ref[...] = jnp.concatenate(
        [pair_lanes(weights, nothing), pair_lanes(nothing, weights)], axis=0
    )


def half_sum(blocks, scale):
    size = blocks.shape[0] // 2
    return (
        blocks[:size, :size] * scale[:, :size] + blocks[size:, size:] * scale[:, size:]
    )


def opposite(way):
    return way + 1 - 2 * lax.rem(way, 2)


def train_kernel(
    rows_count,
    cols_count,
    steps,
    reals_hbm, seed_ref, bank_ref,
    g_in_ref, g_base_ref, g_one_ref, g_two_ref, d_one_ref, d_two_ref, d_out_ref,
    n_in, n_base, n_one, n_two, n_done, n_dtwo, n_dout, verdict_ref,
    small_own, base_own, small_in, base_in,
    cot_own, cot_out, cot_in, scale_own, scale_out, scale_in,
    hidden_s, middle_s, slope_pre_s, slope_mid_s,
    one_b, two_b, one_tb, two_tb, own_one_tb, own_two_tb,
    d1_b, d2_b, d1_tb, d2_tb,
    acc_one, acc_two, acc_feat, sum_done, sum_dtwo, sum_dout,
    latent_s, reals_ref, real_sem,
    fwd_send, fwd_recv, ret_send, ret_recv, sc_send, sc_recv,
):
    places, channels = g_base_ref.shape
    tiles = places // TILE
    my_row = lax.axis_index("row")
    my_col = lax.axis_index("col")

    def device_of(way):
        along = 2 * lax.rem(way, 2) - 1
        vertical = 1 - way // 2
        row = lax.rem(my_row + along * vertical + rows_count, rows_count)
        col = lax.rem(my_col + along * (1 - vertical) + cols_count, cols_count)
        return (row, col)

    def rows_of(tile):
        return pl.ds(pl.multiple_of(tile * TILE, TILE), TILE)

    def small_copy(step, way, slot):
        return pltpu.make_async_remote_copy(
            src_ref=small_own, dst_ref=small_in.at[step, slot],
            send_sem=fwd_send.at[step, way, 0], recv_sem=fwd_recv.at[step, slot, 0],
            device_id=device_of(way), device_id_type=MESH,
        )

    def base_copy(step, way, slot, tile):
        return pltpu.make_async_remote_copy(
            src_ref=base_own.at[rows_of(tile)], dst_ref=base_in.at[step, slot, rows_of(tile)],
            send_sem=fwd_send.at[step, way, tile + 1], recv_sem=fwd_recv.at[step, slot, tile + 1],
            device_id=device_of(way), device_id_type=MESH,
        )

    def cot_copy(step, way, slot, tile):
        return pltpu.make_async_remote_copy(
            src_ref=cot_out.at[step, way, rows_of(tile)],
            dst_ref=cot_in.at[step, slot, rows_of(tile)],
            send_sem=ret_send.at[step, way, tile], recv_sem=ret_recv.at[step, slot, tile],
            device_id=device_of(way), device_id_type=MESH,
        )

    def scale_copy(step, way, slot):
        return pltpu.make_async_remote_copy(
            src_ref=scale_out.at[step, way], dst_ref=scale_in.at[step, slot],
            send_sem=sc_send.at[step, way], recv_sem=sc_recv.at[step, slot],
            device_id=device_of(way), device_id_type=MESH,
        )

    def real_copy(step):
        pair = pl.ds(2 * step, 2)
        return pltpu.make_async_copy(reals_hbm.at[pair], reals_ref.at[pair], real_sem.at[step])

    barrier = pltpu.get_barrier_semaphore()
    for way in range(4):
        pl.semaphore_signal(barrier, inc=1, device_id=device_of(way), device_id_type=MESH)

    for step in range(steps):
        real_copy(step).start()
    n_in[...] = g_in_ref[...]
    n_base[...] = g_base_ref[...]
    n_one[...] = g_one_ref[...]
    n_two[...] = g_two_ref[...]
    n_done[...] = d_one_ref[...]
    n_dtwo[...] = d_two_ref[...]
    n_dout[...] = d_out_ref[...]
    bank_rows = bank_ref.shape[0]
    bank_half = bank_ref[...].astype(bf16)
    at_row = lax.broadcasted_iota(jnp.int32, (8, bank_rows), 0)
    at_lane = lax.broadcasted_iota(jnp.int32, (8, bank_rows), 1)
    for step in range(steps):
        wanted = jnp.where(at_row == 0, seed_ref[step, 0], seed_ref[step, 1])
        chosen = jnp.where((wanted == at_lane) & (at_row < 2), 1.0, 0.0)
        latent_s[step] = dot(chosen.astype(bf16), bank_half)
    verdict_ref[...] = jnp.zeros_like(verdict_ref)
    pl.semaphore_wait(barrier, 4)

    def shifts_of(small):
        hi = small[2 * channels : 2 * channels + 16].astype(f32)
        return hi[0:1] + hi[2:3] + hi[4:5], hi[1:2] + hi[3:4] + hi[5:6]

    def made(base, shift_a, shift_b, one, two, keep):
        base = base.astype(f32)
        gen_pre = pair_lanes(base + shift_a, base + shift_b)
        act, slope = silu_parts(gen_pre)
        hidden = act.astype(bf16)
        middle_pre = dot(hidden, one)
        act_mid, slope_mid = silu_parts(middle_pre)
        middle = act_mid.astype(bf16)
        if keep is not None:
            hidden_s[keep] = hidden
            middle_s[keep] = middle
            slope_pre_s[keep] = slope
            slope_mid_s[keep] = slope_mid
        return (hidden.astype(f32) + dot(middle, two)).astype(bf16)

    def judge_tile(images, d_out_pair):
        first_pre = dot(images, d1_b[...])
        act, slope_first = silu_parts(first_pre)
        first = act.astype(bf16)
        summed = images.astype(f32) + dot(first, d2_b[...])
        feature, slope_sum = silu_parts(summed)
        acc_feat[...] += jnp.sum(feature, axis=0, keepdims=True)
        outer = slope_sum * d_out_pair
        outer_half = outer.astype(bf16)
        inner = (dot(outer_half, d2_tb[...]) * slope_first).astype(bf16)
        acc_two[...] += rows_dot(first, outer_half)
        acc_one[...] += rows_dot(images, inner)
        return outer, inner

    def clear():
        acc_feat[...] = jnp.zeros_like(acc_feat)
        acc_one[...] = jnp.zeros_like(acc_one)
        acc_two[...] = jnp.zeros_like(acc_two)

    def settle(step, place, real):
        feats = acc_feat[...]
        weighted = feats * pair_lanes(n_dout[...], n_dout[...])
        shape = (1, channels)
        low = jnp.sum(weighted[:, :channels], axis=1, keepdims=True) * (1.0 / places)
        high = jnp.sum(weighted[:, channels:], axis=1, keepdims=True) * (1.0 / places)
        low = jnp.broadcast_to(low, shape)
        high = jnp.broadcast_to(high, shape)
        verdict_ref[step, place] = jnp.concatenate(
            [low, high, jnp.zeros((6, channels), f32)], axis=0
        )
        verdict = pair_lanes(low, high)
        against = -sigmoid(-verdict) * (1.0 / places)
        toward = against if real else sigmoid(verdict) * (1.0 / places)
        sum_done[...] += half_sum(acc_one[...], toward)
        sum_dtwo[...] += half_sum(acc_two[...], toward)
        scaled = feats * toward
        sum_dout[...] += scaled[:, :channels] + scaled[:, channels:]
        return jnp.broadcast_to(against, (8, 2 * channels))

    def one_step(step, carry):
        base_own[...] = n_base[...].astype(bf16)
        latent = latent_s[step].astype(bf16)
        shift = dot(latent, n_in[...].astype(bf16))
        top = shift.astype(bf16)
        rest = shift - top.astype(f32)
        mid = rest.astype(bf16)
        last = rest - mid.astype(f32)
        small_own[0:channels] = n_one[...].astype(bf16)
        small_own[channels : 2 * channels] = n_two[...].astype(bf16)
        small_own[2 * channels : 2 * channels + 16] = jnp.concatenate(
            [top[0:2].astype(f32), mid[0:2].astype(f32), last[0:2], jnp.zeros((10, channels), f32)],
            axis=0,
        ).astype(bf16)

        def send_ways(way, carry):
            small_copy(step, way, opposite(way)).start()
            return carry

        def send_bases(at, carry):
            way = lax.rem(at, 4)
            base_copy(step, way, opposite(way), at // 4).start()
            return carry

        lax.fori_loop(0, 4, send_ways, 0)
        lax.fori_loop(0, 4 * tiles, send_bases, 0)

        put_blocks(one_b, n_one[...].astype(bf16))
        put_blocks(two_b, n_two[...].astype(bf16))
        put_blocks(own_one_tb, n_one[...].T.astype(bf16))
        put_blocks(own_two_tb, (0.5 * n_two[...].T).astype(bf16))
        put_blocks(d1_b, n_done[...].astype(bf16))
        put_blocks(d2_b, n_dtwo[...].astype(bf16))
        put_blocks(d1_tb, n_done[...].T.astype(bf16))
        put_blocks(d2_tb, (0.5 * n_dtwo[...].T).astype(bf16))
        sum_done[...] = jnp.zeros_like(sum_done)
        sum_dtwo[...] = jnp.zeros_like(sum_dtwo)
        sum_dout[...] = jnp.zeros_like(sum_dout)
        d_out_pair = 0.5 * pair_lanes(n_dout[...], n_dout[...])

        clear()

        def own_tile(tile, carry):
            at = rows_of(tile)
            images = made(base_own[at], shift[0:1], shift[1:2], one_b[...], two_b[...], at)
            outer, inner = judge_tile(images, d_out_pair)
            cot_own[at] = (outer + dot(inner, d1_tb[...])).astype(bf16)
            return carry

        lax.fori_loop(0, tiles, own_tile, 0)
        scale_own[...] = settle(step, 0, False)

        clear()
        real_copy(step).wait()

        def real_tile(tile, carry):
            at = rows_of(tile)
            judge_tile(pair_lanes(reals_ref[2 * step, at], reals_ref[2 * step + 1, at]), d_out_pair)
            return carry

        lax.fori_loop(0, tiles, real_tile, 0)
        settle(step, 5, True)

        def beside(order, carry):
            way = 3 - order
            small_copy(step, way, way).wait_recv()
            small = small_in.at[step, way]
            put_blocks(one_b, small[0:channels])
            put_blocks(two_b, small[channels : 2 * channels])
            shift_a, shift_b = shifts_of(small)
            clear()

            def their_tile(tile, carry):
                at = rows_of(tile)
                base_copy(step, way, way, tile).wait_recv()
                images = made(base_in[step, way, at], shift_a, shift_b, one_b[...], two_b[...], None)
                outer, inner = judge_tile(images, d_out_pair)
                cot_out[step, way, at] = (outer + dot(inner, d1_tb[...])).astype(bf16)
                cot_copy(step, way, opposite(way), tile).start()
                return carry

            lax.fori_loop(0, tiles, their_tile, 0)
            scale_out[step, way] = settle(step, way + 1, False)
            scale_copy(step, way, opposite(way)).start()
            return carry

        lax.fori_loop(0, 4, beside, 0)

        n_done[...] -= learn_rate * sum_done[...]
        n_dtwo[...] -= learn_rate * sum_dtwo[...]
        n_dout[...] -= learn_rate * sum_dout[...]

        clear()

        def scale_waits(way, carry):
            scale_copy(step, way, way).wait_recv()
            return carry

        lax.fori_loop(0, 4, scale_waits, 0)

        def back_tile(tile, carry):
            at = rows_of(tile)

            def cot_waits(way, carry):
                cot_copy(step, way, way, tile).wait_recv()
                return carry

            lax.fori_loop(0, 4, cot_waits, 0)
            total = cot_own[at].astype(f32) * scale_own[0:1]
            for way in range(4):
                total += cot_in[step, way, at].astype(f32) * scale_in[step, way, 0:1]
            half = total.astype(bf16)
            acc_two[...] += rows_dot(middle_s[at], half)
            inner = (dot(half, own_two_tb[...]) * slope_mid_s[at]).astype(bf16)
            acc_one[...] += rows_dot(hidden_s[at], inner)
            outer = (total + dot(inner, own_one_tb[...])) * slope_pre_s[at]
            acc_feat[...] += jnp.sum(outer, axis=0, keepdims=True)
            n_base[at] -= (0.5 * base_rate * places) * (outer[:, :channels] + outer[:, channels:])
            return carry

        lax.fori_loop(0, tiles, back_tile, 0)
        n_one[...] -= learn_rate * (
            acc_one[:channels, :channels] + acc_one[channels:, channels:]
        )
        n_two[...] -= learn_rate * (
            acc_two[:channels, :channels] + acc_two[channels:, channels:]
        )
        sums = acc_feat[...]
        sums = jnp.concatenate(
            [sums[:, :channels], sums[:, channels:], jnp.zeros((6, channels), f32)], axis=0
        )
        n_in[...] -= (0.5 * learn_rate) * lax.dot_general(
            latent_s[step], sums, (((0,), (0,)), ((), ())),
            precision=lax.Precision.HIGHEST, preferred_element_type=f32,
        )

        def sent(way, carry):
            small_copy(step, way, way).wait_send()
            scale_copy(step, way, way).wait_send()

            def sent_tile(tile, carry):
                base_copy(step, way, way, tile).wait_send()
                cot_copy(step, way, way, tile).wait_send()
                return carry

            return lax.fori_loop(0, tiles, sent_tile, carry)

        lax.fori_loop(0, 4, sent, 0)
        return carry

    lax.fori_loop(0, steps, one_step, 0)


def pick_kernel(index_ref, data_ref, out_ref, sem):
    steps, count = index_ref.shape
    copies = [
        pltpu.make_async_copy(
            data_ref.at[index_ref[i // count, i % count]], out_ref.at[i], sem.at[i]
        )
        for i in range(steps * count)
    ]
    for copy in copies:
        copy.start()
    for copy in copies:
        copy.wait()


def pick(data, index):
    count = index.size
    return pl.pallas_call(
        pick_kernel,
        out_shape=jax.ShapeDtypeStruct((count,) + data.shape[1:], data.dtype),
        in_specs=[
            pl.BlockSpec(memory_space=pltpu.SMEM), pl.BlockSpec(memory_space=pl.ANY)
        ],
        out_specs=pl.BlockSpec(memory_space=pl.ANY),
        scratch_shapes=[pltpu.SemaphoreType.DMA((count,))],
        compiler_params=pltpu.CompilerParams(vmem_limit_bytes=58 * 1024 * 1024),
    )(index, data)


def hand_over_kernel(count, *refs):
    copies = [
        pltpu.make_async_copy(refs[i], refs[count + i], refs[-1].at[i]) for i in range(count)
    ]
    for copy in copies:
        copy.start()
    for copy in copies:
        copy.wait()


def hand_over(members):
    count = len(members)
    anywhere = pl.BlockSpec(memory_space=pl.ANY)
    return pl.pallas_call(
        functools.partial(hand_over_kernel, count),
        out_shape=[jax.ShapeDtypeStruct(member.shape, member.dtype) for member in members],
        in_specs=[anywhere] * count,
        out_specs=[anywhere] * count,
        scratch_shapes=[pltpu.SemaphoreType.DMA((count,))],
    )(*members)


def on_device(
    rows_count, cols_count,
    data, real_index, latent_seed, latent_bank, g_in, g_base, g_one, g_two, d_one, d_two, d_out,
):
    steps = real_index.shape[2]
    places, channels = data.shape[3:]
    reals = pick(data[0, 0], real_index[0, 0])
    wide = 2 * channels
    square = (channels, channels)
    blocks = pltpu.VMEM((wide, wide), bf16)
    tiles = places // TILE
    vmem = pl.BlockSpec(memory_space=pltpu.VMEM)
    small = 2 * channels + 16
    shapes = [square, (places, channels), square, square, square, square, (1, channels)]
    outs = pl.pallas_call(
        functools.partial(train_kernel, rows_count, cols_count, steps),
        out_shape=[jax.ShapeDtypeStruct(shape, f32) for shape in shapes]
        + [jax.ShapeDtypeStruct((steps, 6, 8, channels), f32)],
        in_specs=[pl.BlockSpec(memory_space=pl.ANY), pl.BlockSpec(memory_space=pltpu.SMEM)]
        + [vmem] * 8,
        out_specs=[vmem] * 8,
        scratch_shapes=[
            pltpu.VMEM((small, channels), bf16),
            pltpu.VMEM((places, channels), bf16),
            pltpu.VMEM((steps, 4, small, channels), bf16),
            pltpu.VMEM((steps, 4, places, channels), bf16),
            pltpu.VMEM((places, wide), bf16),
            pltpu.VMEM((steps, 4, places, wide), bf16),
            pltpu.VMEM((steps, 4, places, wide), bf16),
            pltpu.VMEM((8, wide), f32),
            pltpu.VMEM((steps, 4, 8, wide), f32),
            pltpu.VMEM((steps, 4, 8, wide), f32),
            pltpu.VMEM((places, wide), bf16),
            pltpu.VMEM((places, wide), bf16),
            pltpu.VMEM((places, wide), f32),
            pltpu.VMEM((places, wide), f32),
        ]
        + [blocks] * 10
        + [
            pltpu.VMEM((wide, wide), f32),
            pltpu.VMEM((wide, wide), f32),
            pltpu.VMEM((1, wide), f32),
            pltpu.VMEM(square, f32),
            pltpu.VMEM(square, f32),
            pltpu.VMEM((1, channels), f32),
            pltpu.VMEM((steps, 8, channels), f32),
            pltpu.VMEM((2 * steps, places, channels), bf16),
            pltpu.SemaphoreType.DMA((steps,)),
            pltpu.SemaphoreType.DMA((steps, 4, tiles + 1)),
            pltpu.SemaphoreType.DMA((steps, 4, tiles + 1)),
            pltpu.SemaphoreType.DMA((steps, 4, tiles)),
            pltpu.SemaphoreType.DMA((steps, 4, tiles)),
            pltpu.SemaphoreType.DMA((steps, 4)),
            pltpu.SemaphoreType.DMA((steps, 4)),
        ],
        compiler_params=pltpu.CompilerParams(
            collective_id=0, has_side_effects=True, vmem_limit_bytes=50 * 1024 * 1024
        ),
    )(
        reals, latent_seed[0, 0], latent_bank,
        g_in[0, 0], g_base[0, 0], g_one[0, 0], g_two[0, 0], d_one[0, 0], d_two[0, 0],
        d_out.reshape(1, channels),
    )
    verdicts = outs[7][:, :, :2, 0].reshape(1, 1, steps, 12)
    outs = hand_over(outs[:7])
    finals = [member[None, None] for member in outs[:6]] + [outs[6].reshape(1, 1, channels)]
    return (*finals, verdicts)


def solution(mesh):
    whole = P("row", "col", None, None)
    return jax.shard_map(
        functools.partial(on_device, mesh.shape["row"], mesh.shape["col"]),
        mesh=mesh,
        in_specs=(P("row", "col", None, None, None), whole, whole, P()) + (whole,) * 6
        + (P("row", "col", None),),
        out_specs=(whole,) * 6 + (P("row", "col", None), whole),
        check_vma=False,
    )
```

```python
import functools

import jax
import jax.numpy as jnp
from jax import lax
from jax.experimental import pallas as pl
from jax.experimental.pallas import tpu as pltpu
from jax.sharding import PartitionSpec as P

learn_rate = 0.05
base_rate = 0.1

TILE = 512
MESH = pl.DeviceIdType.MESH
f32 = jnp.float32
bf16 = jnp.bfloat16


def dot(left, right):
    return jnp.dot(left, right, preferred_element_type=f32)


def rows_dot(left, right):
    return lax.dot_general(left, right, (((0,), (0,)), ((), ())), preferred_element_type=f32)


def sigmoid(values):
    return 0.5 + 0.5 * jnp.tanh(0.5 * values)


def silu_parts(values):
    half = 0.5 * values
    twice = 1.0 + jnp.tanh(half)
    act = half * twice
    return act, twice * ((1.0 + values) - act)


def pair_lanes(left, right):
    return jnp.concatenate([left, right], axis=1)


def put_blocks(ref, weights):
    size = weights.shape[0]
    nothing = jnp.zeros((size, size), bf16)
    ref[...] = jnp.concatenate(
        [pair_lanes(weights, nothing), pair_lanes(nothing, weights)], axis=0
    )


def half_sum(blocks, scale):
    size = blocks.shape[0] // 2
    return (
        blocks[:size, :size] * scale[:, :size] + blocks[size:, size:] * scale[:, size:]
    )


def train_kernel(
    rows_count,
    cols_count,
    steps,
    reals_ref, seed_ref, bank_ref,
    g_in_ref, g_base_ref, g_one_ref, g_two_ref, d_one_ref, d_two_ref, d_out_ref,
    n_in, n_base, n_one, n_two, n_done, n_dtwo, n_dout, verdict_ref,
    small_own, base_own, small_in, base_in,
    cot_own, cot_out, cot_in, scale_own, scale_out, scale_in,
    hidden_s, middle_s, slope_pre_s, slope_mid_s,
    one_b, two_b, one_tb, two_tb, own_one_tb, own_two_tb,
    d1_b, d2_b, d1_tb, d2_tb,
    acc_one, acc_two, acc_feat, sum_done, sum_dtwo, sum_dout,
    latent_s,
    fwd_send, fwd_recv, ret_send, ret_recv, sc_send, sc_recv,
):
    places, channels = g_base_ref.shape
    tiles = places // TILE
    my_row = lax.axis_index("row")
    my_col = lax.axis_index("col")

    relayed = rows_count == 4
    first_slot = 1 if relayed else 0

    def peer(slot):
        col = lax.rem(my_col + jnp.where(slot == 2, cols_count - 1, 1), cols_count)
        if relayed:
            zero = lax.rem(my_row + 2, 4)
            one = my_row + 1 - 2 * lax.rem(my_row, 2)
        else:
            zero = lax.rem(my_row + rows_count - 1, rows_count)
            one = lax.rem(my_row + 1, rows_count)
        row = jnp.where(slot == 0, zero, jnp.where(slot == 1, one, my_row))
        return (row, jnp.where(slot < 2, my_col, col))

    def far(slot):
        turned = slot + 1 - 2 * lax.rem(slot, 2)
        return jnp.where(slot < 2, slot, turned) if relayed else turned

    def place_of(slot):
        if not relayed:
            return slot + 1
        odd = lax.rem(my_row, 2)
        return jnp.where(slot == 0, 1 + odd, jnp.where(slot == 1, 2 - odd, slot + 1))

    def rows_of(tile):
        return pl.ds(pl.multiple_of(tile * TILE, TILE), TILE)

    def small_copy(step, slot, source):
        return pltpu.make_async_remote_copy(
            src_ref=source, dst_ref=small_in.at[step, far(slot)],
            send_sem=fwd_send.at[step, slot, 0], recv_sem=fwd_recv.at[step, far(slot), 0],
            device_id=peer(slot), device_id_type=MESH,
        )

    def base_copy(step, slot, tile, source):
        return pltpu.make_async_remote_copy(
            src_ref=source, dst_ref=base_in.at[step, far(slot), rows_of(tile)],
            send_sem=fwd_send.at[step, slot, tile + 1],
            recv_sem=fwd_recv.at[step, far(slot), tile + 1],
            device_id=peer(slot), device_id_type=MESH,
        )

    def small_came(step, slot):
        pltpu.make_async_remote_copy(
            src_ref=small_own, dst_ref=small_in.at[step, slot],
            send_sem=fwd_send.at[step, slot, 0], recv_sem=fwd_recv.at[step, slot, 0],
            device_id=peer(slot), device_id_type=MESH,
        ).wait_recv()

    def base_came(step, slot, tile):
        pltpu.make_async_remote_copy(
            src_ref=base_own.at[rows_of(tile)], dst_ref=base_in.at[step, slot, rows_of(tile)],
            send_sem=fwd_send.at[step, slot, tile + 1], recv_sem=fwd_recv.at[step, slot, tile + 1],
            device_id=peer(slot), device_id_type=MESH,
        ).wait_recv()

    def cot_copy(step, slot, there, tile):
        return pltpu.make_async_remote_copy(
            src_ref=cot_out.at[step, slot, rows_of(tile)],
            dst_ref=cot_in.at[step, there, rows_of(tile)],
            send_sem=ret_send.at[step, slot, tile], recv_sem=ret_recv.at[step, there, tile],
            device_id=peer(slot), device_id_type=MESH,
        )

    def scale_copy(step, slot, there):
        return pltpu.make_async_remote_copy(
            src_ref=scale_out.at[step, slot], dst_ref=scale_in.at[step, there],
            send_sem=sc_send.at[step, slot], recv_sem=sc_recv.at[step, there],
            device_id=peer(slot), device_id_type=MESH,
        )

    barrier = pltpu.get_barrier_semaphore()
    for slot in range(4):
        pl.semaphore_signal(barrier, inc=1, device_id=peer(slot), device_id_type=MESH)

    n_in[...] = g_in_ref[...]
    n_base[...] = g_base_ref[...]
    n_one[...] = g_one_ref[...]
    n_two[...] = g_two_ref[...]
    n_done[...] = d_one_ref[...]
    n_dtwo[...] = d_two_ref[...]
    n_dout[...] = d_out_ref[...]
    bank_rows = bank_ref.shape[0]
    bank_half = bank_ref[...].astype(bf16)
    at_row = lax.broadcasted_iota(jnp.int32, (8, bank_rows), 0)
    at_lane = lax.broadcasted_iota(jnp.int32, (8, bank_rows), 1)
    for step in range(steps):
        wanted = jnp.where(at_row == 0, seed_ref[step, 0], seed_ref[step, 1])
        chosen = jnp.where((wanted == at_lane) & (at_row < 2), 1.0, 0.0)
        latent_s[step] = dot(chosen.astype(bf16), bank_half)
    verdict_ref[...] = jnp.zeros_like(verdict_ref)
    pl.semaphore_wait(barrier, 4)

    def shifts_of(small):
        hi = small[2 * channels : 2 * channels + 16].astype(f32)
        return hi[0:1] + hi[2:3] + hi[4:5], hi[1:2] + hi[3:4] + hi[5:6]

    def made(base, shift_a, shift_b, one, two, keep):
        base = base.astype(f32)
        gen_pre = pair_lanes(base + shift_a, base + shift_b)
        act, slope = silu_parts(gen_pre)
        hidden = act.astype(bf16)
        middle_pre = dot(hidden, one)
        act_mid, slope_mid = silu_parts(middle_pre)
        middle = act_mid.astype(bf16)
        if keep is not None:
            hidden_s[keep] = hidden
            middle_s[keep] = middle
            slope_pre_s[keep] = slope
            slope_mid_s[keep] = slope_mid
        return (hidden.astype(f32) + dot(middle, two)).astype(bf16)

    def judge_tile(images, d_out_pair):
        first_pre = dot(images, d1_b[...])
        act, slope_first = silu_parts(first_pre)
        first = act.astype(bf16)
        summed = images.astype(f32) + dot(first, d2_b[...])
        feature, slope_sum = silu_parts(summed)
        acc_feat[...] += jnp.sum(feature, axis=0, keepdims=True)
        outer = slope_sum * d_out_pair
        outer_half = outer.astype(bf16)
        inner = (dot(outer_half, d2_tb[...]) * slope_first).astype(bf16)
        acc_two[...] += rows_dot(first, outer_half)
        acc_one[...] += rows_dot(images, inner)
        return outer, inner

    def clear():
        acc_feat[...] = jnp.zeros_like(acc_feat)
        acc_one[...] = jnp.zeros_like(acc_one)
        acc_two[...] = jnp.zeros_like(acc_two)

    def settle(step, place, real):
        feats = acc_feat[...]
        weighted = feats * pair_lanes(n_dout[...], n_dout[...])
        shape = (1, channels)
        low = jnp.sum(weighted[:, :channels], axis=1, keepdims=True) * (1.0 / places)
        high = jnp.sum(weighted[:, channels:], axis=1, keepdims=True) * (1.0 / places)
        low = jnp.broadcast_to(low, shape)
        high = jnp.broadcast_to(high, shape)
        verdict_ref[step, place] = jnp.concatenate(
            [low, high, jnp.zeros((6, channels), f32)], axis=0
        )
        verdict = pair_lanes(low, high)
        against = -sigmoid(-verdict) * (1.0 / places)
        toward = against if real else sigmoid(verdict) * (1.0 / places)
        sum_done[...] += half_sum(acc_one[...], toward)
        sum_dtwo[...] += half_sum(acc_two[...], toward)
        scaled = feats * toward
        sum_dout[...] += scaled[:, :channels] + scaled[:, channels:]
        return jnp.broadcast_to(against, (8, 2 * channels))

    def one_step(step, carry):
        base_own[...] = n_base[...].astype(bf16)
        latent = latent_s[step].astype(bf16)
        shift = dot(latent, n_in[...].astype(bf16))
        top = shift.astype(bf16)
        rest = shift - top.astype(f32)
        mid = rest.astype(bf16)
        last = rest - mid.astype(f32)
        small_own[0:channels] = n_one[...].astype(bf16)
        small_own[channels : 2 * channels] = n_two[...].astype(bf16)
        small_own[2 * channels : 2 * channels + 16] = jnp.concatenate(
            [top[0:2].astype(f32), mid[0:2].astype(f32), last[0:2], jnp.zeros((10, channels), f32)],
            axis=0,
        ).astype(bf16)

        def send_smalls(slot, carry):
            small_copy(step, slot, small_own).start()
            return carry

        def send_bases(tile, carry):
            def send(slot, carry):
                base_copy(step, slot, tile, base_own.at[rows_of(tile)]).start()
                return carry

            return lax.fori_loop(first_slot, 4, send, carry)

        def pass_on(tile):
            if relayed:
                @pl.when(tile == 0)
                def _():
                    small_came(step, 1)
                    small_copy(step, 0, small_in.at[step, 1]).start()

                @pl.when(tile < tiles)
                def _():
                    base_came(step, 1, tile)
                    base_copy(step, 0, tile, base_in.at[step, 1, rows_of(tile)]).start()

        lax.fori_loop(first_slot, 4, send_smalls, 0)
        lax.fori_loop(0, tiles, send_bases, 0)

        put_blocks(one_b, n_one[...].astype(bf16))
        put_blocks(two_b, n_two[...].astype(bf16))
        put_blocks(own_one_tb, n_one[...].T.astype(bf16))
        put_blocks(own_two_tb, (0.5 * n_two[...].T).astype(bf16))
        put_blocks(d1_b, n_done[...].astype(bf16))
        put_blocks(d2_b, n_dtwo[...].astype(bf16))
        put_blocks(d1_tb, n_done[...].T.astype(bf16))
        put_blocks(d2_tb, (0.5 * n_dtwo[...].T).astype(bf16))
        sum_done[...] = jnp.zeros_like(sum_done)
        sum_dtwo[...] = jnp.zeros_like(sum_dtwo)
        sum_dout[...] = jnp.zeros_like(sum_dout)
        d_out_pair = 0.5 * pair_lanes(n_dout[...], n_dout[...])

        clear()

        def own_tile(tile, carry):
            at = rows_of(tile)
            images = made(base_own[at], shift[0:1], shift[1:2], one_b[...], two_b[...], at)
            outer, inner = judge_tile(images, d_out_pair)
            cot_own[at] = (outer + dot(inner, d1_tb[...])).astype(bf16)
            return carry

        lax.fori_loop(0, tiles, own_tile, 0)
        scale_own[...] = settle(step, 0, False)

        pass_on(jnp.int32(0))

        clear()

        def real_tile(tile, carry):
            at = rows_of(tile)
            judge_tile(pair_lanes(reals_ref[2 * step, at], reals_ref[2 * step + 1, at]), d_out_pair)
            pass_on(tile + 1)
            return carry

        lax.fori_loop(0, tiles, real_tile, 0)
        settle(step, 5, True)

        def add_partner(tile):
            @pl.when(tile == 0)
            def _():
                scale_copy(step, 0, 0).wait_recv()

            at = rows_of(tile)
            cot_copy(step, 0, 0, tile).wait_recv()
            total = cot_out[step, 1, at].astype(f32) * scale_out[step, 1, 0:1]
            total += cot_in[step, 0, at].astype(f32) * scale_in[step, 0, 0:1]
            cot_out[step, 1, at] = total.astype(bf16)
            cot_copy(step, 1, 1, tile).start()

        def beside(slot, carry):
            def came():
                small_came(step, slot)

            if relayed:
                pl.when(slot != 1)(came)
            else:
                came()
            small = small_in.at[step, slot]
            put_blocks(one_b, small[0:channels])
            put_blocks(two_b, small[channels : 2 * channels])
            shift_a, shift_b = shifts_of(small)
            clear()

            def their_tile(tile, carry):
                at = rows_of(tile)

                def came():
                    base_came(step, slot, tile)

                def back():
                    cot_copy(step, slot, far(slot), tile).start()

                if relayed:
                    pl.when(slot != 1)(came)
                else:
                    came()
                images = made(base_in[step, slot, at], shift_a, shift_b, one_b[...], two_b[...], None)
                outer, inner = judge_tile(images, d_out_pair)
                cot_out[step, slot, at] = (outer + dot(inner, d1_tb[...])).astype(bf16)
                if relayed:
                    pl.when(slot != 1)(back)
                    pl.when(slot == 2)(lambda: add_partner(tile))
                else:
                    back()
                return carry

            lax.fori_loop(0, tiles, their_tile, 0)
            scale_out[step, slot] = settle(step, place_of(slot), False)

            def back_scale():
                scale_copy(step, slot, far(slot)).start()

            if relayed:
                pl.when(slot != 1)(back_scale)
            else:
                back_scale()
            return carry

        lax.fori_loop(0, 4, beside, 0)

        n_done[...] -= learn_rate * sum_done[...]
        n_dtwo[...] -= learn_rate * sum_dtwo[...]
        n_dout[...] -= learn_rate * sum_dout[...]

        clear()

        def scale_waits(slot, carry):
            scale_copy(step, slot, slot).wait_recv()
            return carry

        lax.fori_loop(2 if relayed else 0, 4, scale_waits, 0)

        def back_tile(tile, carry):
            at = rows_of(tile)

            def cot_waits(slot, carry):
                cot_copy(step, slot, slot, tile).wait_recv()
                return carry

            lax.fori_loop(first_slot, 4, cot_waits, 0)
            total = cot_own[at].astype(f32) * scale_own[0:1]
            if relayed:
                total += cot_in[step, 1, at].astype(f32)
            for slot in range(2 if relayed else 0, 4):
                total += cot_in[step, slot, at].astype(f32) * scale_in[step, slot, 0:1]
            half = total.astype(bf16)
            acc_two[...] += rows_dot(middle_s[at], half)
            inner = (dot(half, own_two_tb[...]) * slope_mid_s[at]).astype(bf16)
            acc_one[...] += rows_dot(hidden_s[at], inner)
            outer = (total + dot(inner, own_one_tb[...])) * slope_pre_s[at]
            acc_feat[...] += jnp.sum(outer, axis=0, keepdims=True)
            n_base[at] -= (0.5 * base_rate * places) * (outer[:, :channels] + outer[:, channels:])
            return carry

        lax.fori_loop(0, tiles, back_tile, 0)
        n_one[...] -= learn_rate * (
            acc_one[:channels, :channels] + acc_one[channels:, channels:]
        )
        n_two[...] -= learn_rate * (
            acc_two[:channels, :channels] + acc_two[channels:, channels:]
        )
        sums = acc_feat[...]
        sums = jnp.concatenate(
            [sums[:, :channels], sums[:, channels:], jnp.zeros((6, channels), f32)], axis=0
        )
        n_in[...] -= (0.5 * learn_rate) * lax.dot_general(
            latent_s[step], sums, (((0,), (0,)), ((), ())),
            precision=lax.Precision.HIGHEST, preferred_element_type=f32,
        )

        def sent(slot, carry):
            small_copy(step, slot, small_own).wait_send()

            def scale_sent():
                scale_copy(step, slot, far(slot)).wait_send()

            if relayed:
                pl.when(slot != 1)(scale_sent)
            else:
                scale_sent()

            def sent_tile(tile, carry):
                base_copy(step, slot, tile, base_own.at[rows_of(tile)]).wait_send()
                cot_copy(step, slot, far(slot), tile).wait_send()
                return carry

            return lax.fori_loop(0, tiles, sent_tile, carry)

        lax.fori_loop(0, 4, sent, 0)
        return carry

    lax.fori_loop(0, steps, one_step, 0)


def pick_kernel(index_ref, data_ref, out_ref, sem):
    steps, count = index_ref.shape
    copies = [
        pltpu.make_async_copy(
            data_ref.at[index_ref[i // count, i % count]], out_ref.at[i], sem.at[i]
        )
        for i in range(steps * count)
    ]
    for copy in copies:
        copy.start()
    for copy in copies:
        copy.wait()


def pick(data, index):
    count = index.size
    return pl.pallas_call(
        pick_kernel,
        out_shape=jax.ShapeDtypeStruct((count,) + data.shape[1:], data.dtype),
        in_specs=[
            pl.BlockSpec(memory_space=pltpu.SMEM), pl.BlockSpec(memory_space=pl.ANY)
        ],
        out_specs=pl.BlockSpec(memory_space=pltpu.VMEM),
        scratch_shapes=[pltpu.SemaphoreType.DMA((count,))],
        compiler_params=pltpu.CompilerParams(vmem_limit_bytes=58 * 1024 * 1024),
    )(index, data)


def hand_over_kernel(count, *refs):
    for i in range(count):
        refs[count + i][...] = refs[i][...]


def hand_over(members):
    count = len(members)
    vmem = pl.BlockSpec(memory_space=pltpu.VMEM)
    return pl.pallas_call(
        functools.partial(hand_over_kernel, count),
        out_shape=[jax.ShapeDtypeStruct(member.shape, member.dtype) for member in members],
        in_specs=[vmem] * count,
        out_specs=[vmem] * count,
    )(*members)


def on_device(
    rows_count, cols_count,
    data, real_index, latent_seed, latent_bank, g_in, g_base, g_one, g_two, d_one, d_two, d_out,
):
    steps = real_index.shape[2]
    places, channels = data.shape[3:]
    reals = pick(data[0, 0], real_index[0, 0])
    wide = 2 * channels
    square = (channels, channels)
    blocks = pltpu.VMEM((wide, wide), bf16)
    tiles = places // TILE
    vmem = pl.BlockSpec(memory_space=pltpu.VMEM)
    small = 2 * channels + 16
    shapes = [square, (places, channels), square, square, square, square, (1, channels)]
    outs = pl.pallas_call(
        functools.partial(train_kernel, rows_count, cols_count, steps),
        out_shape=[jax.ShapeDtypeStruct(shape, f32) for shape in shapes]
        + [jax.ShapeDtypeStruct((steps, 6, 8, channels), f32)],
        in_specs=[vmem, pl.BlockSpec(memory_space=pltpu.SMEM)] + [vmem] * 8,
        out_specs=[vmem] * 8,
        scratch_shapes=[
            pltpu.VMEM((small, channels), bf16),
            pltpu.VMEM((places, channels), bf16),
            pltpu.VMEM((steps, 4, small, channels), bf16),
            pltpu.VMEM((steps, 4, places, channels), bf16),
            pltpu.VMEM((places, wide), bf16),
            pltpu.VMEM((steps, 4, places, wide), bf16),
            pltpu.VMEM((steps, 4, places, wide), bf16),
            pltpu.VMEM((8, wide), f32),
            pltpu.VMEM((steps, 4, 8, wide), f32),
            pltpu.VMEM((steps, 4, 8, wide), f32),
            pltpu.VMEM((places, wide), bf16),
            pltpu.VMEM((places, wide), bf16),
            pltpu.VMEM((places, wide), f32),
            pltpu.VMEM((places, wide), f32),
        ]
        + [blocks] * 10
        + [
            pltpu.VMEM((wide, wide), f32),
            pltpu.VMEM((wide, wide), f32),
            pltpu.VMEM((1, wide), f32),
            pltpu.VMEM(square, f32),
            pltpu.VMEM(square, f32),
            pltpu.VMEM((1, channels), f32),
            pltpu.VMEM((steps, 8, channels), f32),
            pltpu.SemaphoreType.DMA((steps, 4, tiles + 1)),
            pltpu.SemaphoreType.DMA((steps, 4, tiles + 1)),
            pltpu.SemaphoreType.DMA((steps, 4, tiles)),
            pltpu.SemaphoreType.DMA((steps, 4, tiles)),
            pltpu.SemaphoreType.DMA((steps, 4)),
            pltpu.SemaphoreType.DMA((steps, 4)),
        ],
        compiler_params=pltpu.CompilerParams(
            collective_id=0, has_side_effects=True, vmem_limit_bytes=50 * 1024 * 1024
        ),
    )(
        reals, latent_seed[0, 0], latent_bank,
        g_in[0, 0], g_base[0, 0], g_one[0, 0], g_two[0, 0], d_one[0, 0], d_two[0, 0],
        d_out.reshape(1, channels),
    )
    verdicts = outs[7][:, :, :2, 0].reshape(1, 1, steps, 12)
    outs = hand_over(outs[:7])
    finals = [member[None, None] for member in outs[:6]] + [outs[6].reshape(1, 1, channels)]
    return (*finals, verdicts)


def solution(mesh):
    whole = P("row", "col", None, None)
    return jax.shard_map(
        functools.partial(on_device, mesh.shape["row"], mesh.shape["col"]),
        mesh=mesh,
        in_specs=(P("row", "col", None, None, None), whole, whole, P()) + (whole,) * 6
        + (P("row", "col", None),),
        out_specs=(whole,) * 6 + (P("row", "col", None), whole),
        check_vma=False,
    )
```

```python
import functools

import jax
import jax.numpy as jnp
from jax import lax
from jax.experimental import pallas as pl
from jax.experimental.pallas import tpu as pltpu
from jax.sharding import PartitionSpec as P

learn_rate = 0.05
base_rate = 0.1

TILE = 512
SLAB = 32
MESH = pl.DeviceIdType.MESH
f32 = jnp.float32
bf16 = jnp.bfloat16


def dot(left, right):
    return jnp.dot(left, right, preferred_element_type=f32)


def rows_dot(left, right):
    return lax.dot_general(left, right, (((0,), (0,)), ((), ())), preferred_element_type=f32)


def sigmoid(values):
    return 0.5 + 0.5 * jnp.tanh(0.5 * values)


def silu_parts(values):
    half = 0.5 * values
    twice = 1.0 + jnp.tanh(half)
    act = half * twice
    return act, twice * ((1.0 + values) - act)


def by_slabs(function, *arrays):
    parts = [
        function(*(member[at : at + SLAB] for member in arrays))
        for at in range(0, arrays[0].shape[0], SLAB)
    ]
    return tuple(jnp.concatenate(list(piece), axis=0) for piece in zip(*parts))


def pair_lanes(left, right):
    return jnp.concatenate([left, right], axis=1)


def put_blocks(ref, weights):
    size = weights.shape[0]
    nothing = jnp.zeros((size, size), bf16)
    ref[...] = jnp.concatenate(
        [pair_lanes(weights, nothing), pair_lanes(nothing, weights)], axis=0
    )


def half_sum(blocks, scale):
    size = blocks.shape[0] // 2
    return (
        blocks[:size, :size] * scale[:, :size] + blocks[size:, size:] * scale[:, size:]
    )


def train_kernel(
    rows_count,
    cols_count,
    steps,
    reals_ref, seed_ref, bank_ref,
    g_in_ref, g_base_ref, g_one_ref, g_two_ref, d_one_ref, d_two_ref, d_out_ref,
    n_in, n_base, n_one, n_two, n_done, n_dtwo, n_dout, verdict_ref,
    small_own, base_own, small_in, base_in,
    cot_own, cot_out, cot_in, scale_own, scale_out, scale_in,
    hidden_s, middle_s, slope_pre_s, slope_mid_s,
    one_b, two_b, one_tb, two_tb, own_one_tb, own_two_tb,
    d1_b, d2_b, d1_tb, d2_tb,
    acc_one, acc_two, acc_feat, sum_done, sum_dtwo, sum_dout,
    latent_s,
    fwd_send, fwd_recv, ret_send, ret_recv, sc_send, sc_recv,
):
    places, channels = g_base_ref.shape
    tiles = places // TILE
    my_row = lax.axis_index("row")
    my_col = lax.axis_index("col")

    relayed = rows_count == 4
    first_slot = 1 if relayed else 0

    def peer(slot):
        col = lax.rem(my_col + jnp.where(slot == 2, cols_count - 1, 1), cols_count)
        if relayed:
            zero = lax.rem(my_row + 2, 4)
            one = my_row + 1 - 2 * lax.rem(my_row, 2)
        else:
            zero = lax.rem(my_row + rows_count - 1, rows_count)
            one = lax.rem(my_row + 1, rows_count)
        row = jnp.where(slot == 0, zero, jnp.where(slot == 1, one, my_row))
        return (row, jnp.where(slot < 2, my_col, col))

    def far(slot):
        turned = slot + 1 - 2 * lax.rem(slot, 2)
        return jnp.where(slot < 2, slot, turned) if relayed else turned

    def place_of(slot):
        if not relayed:
            return slot + 1
        odd = lax.rem(my_row, 2)
        return jnp.where(slot == 0, 1 + odd, jnp.where(slot == 1, 2 - odd, slot + 1))

    def rows_of(tile):
        return pl.ds(pl.multiple_of(tile * TILE, TILE), TILE)

    def small_copy(step, slot, source):
        return pltpu.make_async_remote_copy(
            src_ref=source, dst_ref=small_in.at[step, far(slot)],
            send_sem=fwd_send.at[step, slot, 0], recv_sem=fwd_recv.at[step, far(slot), 0],
            device_id=peer(slot), device_id_type=MESH,
        )

    def base_copy(step, slot, tile, source):
        return pltpu.make_async_remote_copy(
            src_ref=source, dst_ref=base_in.at[step, far(slot), rows_of(tile)],
            send_sem=fwd_send.at[step, slot, tile + 1],
            recv_sem=fwd_recv.at[step, far(slot), tile + 1],
            device_id=peer(slot), device_id_type=MESH,
        )

    def small_came(step, slot):
        pltpu.make_async_remote_copy(
            src_ref=small_own, dst_ref=small_in.at[step, slot],
            send_sem=fwd_send.at[step, slot, 0], recv_sem=fwd_recv.at[step, slot, 0],
            device_id=peer(slot), device_id_type=MESH,
        ).wait_recv()

    def base_came(step, slot, tile):
        pltpu.make_async_remote_copy(
            src_ref=base_own.at[rows_of(tile)], dst_ref=base_in.at[step, slot, rows_of(tile)],
            send_sem=fwd_send.at[step, slot, tile + 1], recv_sem=fwd_recv.at[step, slot, tile + 1],
            device_id=peer(slot), device_id_type=MESH,
        ).wait_recv()

    def cot_copy(step, slot, there, tile):
        return pltpu.make_async_remote_copy(
            src_ref=cot_out.at[step, slot, rows_of(tile)],
            dst_ref=cot_in.at[step, there, rows_of(tile)],
            send_sem=ret_send.at[step, slot, tile], recv_sem=ret_recv.at[step, there, tile],
            device_id=peer(slot), device_id_type=MESH,
        )

    def scale_copy(step, slot, there):
        return pltpu.make_async_remote_copy(
            src_ref=scale_out.at[step, slot], dst_ref=scale_in.at[step, there],
            send_sem=sc_send.at[step, slot], recv_sem=sc_recv.at[step, there],
            device_id=peer(slot), device_id_type=MESH,
        )

    barrier = pltpu.get_barrier_semaphore()
    for slot in range(4):
        pl.semaphore_signal(barrier, inc=1, device_id=peer(slot), device_id_type=MESH)

    n_in[...] = g_in_ref[...]
    n_base[...] = g_base_ref[...]
    n_one[...] = g_one_ref[...]
    n_two[...] = g_two_ref[...]
    n_done[...] = d_one_ref[...]
    n_dtwo[...] = d_two_ref[...]
    n_dout[...] = d_out_ref[...]
    bank_rows = bank_ref.shape[0]
    bank_half = bank_ref[...].astype(bf16)
    at_row = lax.broadcasted_iota(jnp.int32, (8, bank_rows), 0)
    at_lane = lax.broadcasted_iota(jnp.int32, (8, bank_rows), 1)
    for step in range(steps):
        wanted = jnp.where(at_row == 0, seed_ref[step, 0], seed_ref[step, 1])
        chosen = jnp.where((wanted == at_lane) & (at_row < 2), 1.0, 0.0)
        latent_s[step] = dot(chosen.astype(bf16), bank_half)
    verdict_ref[...] = jnp.zeros_like(verdict_ref)
    pl.semaphore_wait(barrier, 4)

    def shifts_of(small):
        hi = small[2 * channels : 2 * channels + 16].astype(f32)
        return hi[0:1] + hi[2:3] + hi[4:5], hi[1:2] + hi[3:4] + hi[5:6]

    def made(base, shift_a, shift_b, one, two, keep):
        def enter(rows):
            rows = rows.astype(f32)
            act, slope = silu_parts(pair_lanes(rows + shift_a, rows + shift_b))
            return act.astype(bf16), slope

        def halfway(rows):
            act, slope = silu_parts(rows)
            return act.astype(bf16), slope

        def leave(hidden_rows, rows):
            return ((hidden_rows.astype(f32) + rows).astype(bf16),)

        hidden, slope = by_slabs(enter, base)
        middle, slope_mid = by_slabs(halfway, dot(hidden, one))
        if keep is not None:
            hidden_s[keep] = hidden
            middle_s[keep] = middle
            slope_pre_s[keep] = slope
            slope_mid_s[keep] = slope_mid
        return by_slabs(leave, hidden, dot(middle, two))[0]

    def judge_tile(images, d_out_pair):
        def halfway(rows):
            act, slope = silu_parts(rows)
            return act.astype(bf16), slope

        def leave(image_rows, rows):
            feature, slope = silu_parts(image_rows.astype(f32) + rows)
            outer = slope * d_out_pair
            return outer, outer.astype(bf16), jnp.sum(
                feature.reshape(SLAB // 8, 8, 2 * channels), axis=0
            )

        def turn(rows, slope):
            return ((rows * slope).astype(bf16),)

        first, slope_first = by_slabs(halfway, dot(images, d1_b[...]))
        outer, outer_half, feature_sums = by_slabs(leave, images, dot(first, d2_b[...]))
        acc_feat[...] += jnp.sum(feature_sums, axis=0, keepdims=True)
        inner = by_slabs(turn, dot(outer_half, d2_tb[...]), slope_first)[0]
        acc_two[...] += rows_dot(first, outer_half)
        acc_one[...] += rows_dot(images, inner)
        return outer, inner

    def returned(outer, inner):
        def add(outer_rows, rows):
            return ((outer_rows + rows).astype(bf16),)

        return by_slabs(add, outer, dot(inner, d1_tb[...]))[0]

    def clear():
        acc_feat[...] = jnp.zeros_like(acc_feat)
        acc_one[...] = jnp.zeros_like(acc_one)
        acc_two[...] = jnp.zeros_like(acc_two)

    def settle(step, place, real):
        feats = acc_feat[...]
        weighted = feats * pair_lanes(n_dout[...], n_dout[...])
        shape = (1, channels)
        low = jnp.sum(weighted[:, :channels], axis=1, keepdims=True) * (1.0 / places)
        high = jnp.sum(weighted[:, channels:], axis=1, keepdims=True) * (1.0 / places)
        low = jnp.broadcast_to(low, shape)
        high = jnp.broadcast_to(high, shape)
        verdict_ref[step, place] = jnp.concatenate(
            [low, high, jnp.zeros((6, channels), f32)], axis=0
        )
        verdict = pair_lanes(low, high)
        against = -sigmoid(-verdict) * (1.0 / places)
        toward = against if real else sigmoid(verdict) * (1.0 / places)
        sum_done[...] += half_sum(acc_one[...], toward)
        sum_dtwo[...] += half_sum(acc_two[...], toward)
        scaled = feats * toward
        sum_dout[...] += scaled[:, :channels] + scaled[:, channels:]
        return jnp.broadcast_to(against, (8, 2 * channels))

    def one_step(step, carry):
        base_own[...] = n_base[...].astype(bf16)
        latent = latent_s[step].astype(bf16)
        shift = dot(latent, n_in[...].astype(bf16))
        top = shift.astype(bf16)
        rest = shift - top.astype(f32)
        mid = rest.astype(bf16)
        last = rest - mid.astype(f32)
        small_own[0:channels] = n_one[...].astype(bf16)
        small_own[channels : 2 * channels] = n_two[...].astype(bf16)
        small_own[2 * channels : 2 * channels + 16] = jnp.concatenate(
            [top[0:2].astype(f32), mid[0:2].astype(f32), last[0:2], jnp.zeros((10, channels), f32)],
            axis=0,
        ).astype(bf16)

        def send_smalls(slot, carry):
            small_copy(step, slot, small_own).start()
            return carry

        def send_bases(tile, carry):
            def send(slot, carry):
                base_copy(step, slot, tile, base_own.at[rows_of(tile)]).start()
                return carry

            return lax.fori_loop(first_slot, 4, send, carry)

        def pass_on(tile):
            if relayed:
                @pl.when(tile == 0)
                def _():
                    small_came(step, 1)
                    small_copy(step, 0, small_in.at[step, 1]).start()

                @pl.when(tile < tiles)
                def _():
                    base_came(step, 1, tile)
                    base_copy(step, 0, tile, base_in.at[step, 1, rows_of(tile)]).start()

        lax.fori_loop(first_slot, 4, send_smalls, 0)
        lax.fori_loop(0, tiles, send_bases, 0)

        put_blocks(one_b, n_one[...].astype(bf16))
        put_blocks(two_b, n_two[...].astype(bf16))
        put_blocks(own_one_tb, n_one[...].T.astype(bf16))
        put_blocks(own_two_tb, (0.5 * n_two[...].T).astype(bf16))
        put_blocks(d1_b, n_done[...].astype(bf16))
        put_blocks(d2_b, n_dtwo[...].astype(bf16))
        put_blocks(d1_tb, n_done[...].T.astype(bf16))
        put_blocks(d2_tb, (0.5 * n_dtwo[...].T).astype(bf16))
        sum_done[...] = jnp.zeros_like(sum_done)
        sum_dtwo[...] = jnp.zeros_like(sum_dtwo)
        sum_dout[...] = jnp.zeros_like(sum_dout)
        d_out_pair = 0.5 * pair_lanes(n_dout[...], n_dout[...])

        clear()

        def own_tile(tile, carry):
            at = rows_of(tile)
            images = made(base_own[at], shift[0:1], shift[1:2], one_b[...], two_b[...], at)
            outer, inner = judge_tile(images, d_out_pair)
            cot_own[at] = returned(outer, inner)
            return carry

        lax.fori_loop(0, tiles, own_tile, 0)
        scale_own[...] = settle(step, 0, False)

        pass_on(jnp.int32(0))

        clear()

        def real_tile(tile, carry):
            at = rows_of(tile)
            judge_tile(pair_lanes(reals_ref[2 * step, at], reals_ref[2 * step + 1, at]), d_out_pair)
            pass_on(tile + 1)
            return carry

        lax.fori_loop(0, tiles, real_tile, 0)
        settle(step, 5, True)

        def add_partner(tile):
            @pl.when(tile == 0)
            def _():
                scale_copy(step, 0, 0).wait_recv()

            at = rows_of(tile)
            cot_copy(step, 0, 0, tile).wait_recv()
            total = cot_out[step, 1, at].astype(f32) * scale_out[step, 1, 0:1]
            total += cot_in[step, 0, at].astype(f32) * scale_in[step, 0, 0:1]
            cot_out[step, 1, at] = total.astype(bf16)
            cot_copy(step, 1, 1, tile).start()

        def beside(slot, carry):
            def came():
                small_came(step, slot)

            if relayed:
                pl.when(slot != 1)(came)
            else:
                came()
            small = small_in.at[step, slot]
            put_blocks(one_b, small[0:channels])
            put_blocks(two_b, small[channels : 2 * channels])
            shift_a, shift_b = shifts_of(small)
            clear()

            def their_tile(tile, carry):
                at = rows_of(tile)

                def came():
                    base_came(step, slot, tile)

                def back():
                    cot_copy(step, slot, far(slot), tile).start()

                if relayed:
                    pl.when(slot != 1)(came)
                else:
                    came()
                images = made(base_in[step, slot, at], shift_a, shift_b, one_b[...], two_b[...], None)
                outer, inner = judge_tile(images, d_out_pair)
                cot_out[step, slot, at] = returned(outer, inner)
                if relayed:
                    pl.when(slot != 1)(back)
                    pl.when(slot == 2)(lambda: add_partner(tile))
                else:
                    back()
                return carry

            lax.fori_loop(0, tiles, their_tile, 0)
            scale_out[step, slot] = settle(step, place_of(slot), False)

            def back_scale():
                scale_copy(step, slot, far(slot)).start()

            if relayed:
                pl.when(slot != 1)(back_scale)
            else:
                back_scale()
            return carry

        lax.fori_loop(0, 4, beside, 0)

        n_done[...] -= learn_rate * sum_done[...]
        n_dtwo[...] -= learn_rate * sum_dtwo[...]
        n_dout[...] -= learn_rate * sum_dout[...]

        clear()

        def scale_waits(slot, carry):
            scale_copy(step, slot, slot).wait_recv()
            return carry

        lax.fori_loop(2 if relayed else 0, 4, scale_waits, 0)

        def back_tile(tile, carry):
            at = rows_of(tile)

            def cot_waits(slot, carry):
                cot_copy(step, slot, slot, tile).wait_recv()
                return carry

            lax.fori_loop(first_slot, 4, cot_waits, 0)
            total = cot_own[at].astype(f32) * scale_own[0:1]
            if relayed:
                total += cot_in[step, 1, at].astype(f32)
            for slot in range(2 if relayed else 0, 4):
                total += cot_in[step, slot, at].astype(f32) * scale_in[step, slot, 0:1]
            half = total.astype(bf16)
            acc_two[...] += rows_dot(middle_s[at], half)
            inner = (dot(half, own_two_tb[...]) * slope_mid_s[at]).astype(bf16)
            acc_one[...] += rows_dot(hidden_s[at], inner)
            outer = (total + dot(inner, own_one_tb[...])) * slope_pre_s[at]
            acc_feat[...] += jnp.sum(outer, axis=0, keepdims=True)
            n_base[at] -= (0.5 * base_rate * places) * (outer[:, :channels] + outer[:, channels:])
            return carry

        lax.fori_loop(0, tiles, back_tile, 0)
        n_one[...] -= learn_rate * (
            acc_one[:channels, :channels] + acc_one[channels:, channels:]
        )
        n_two[...] -= learn_rate * (
            acc_two[:channels, :channels] + acc_two[channels:, channels:]
        )
        sums = acc_feat[...]
        sums = jnp.concatenate(
            [sums[:, :channels], sums[:, channels:], jnp.zeros((6, channels), f32)], axis=0
        )
        n_in[...] -= (0.5 * learn_rate) * lax.dot_general(
            latent_s[step], sums, (((0,), (0,)), ((), ())),
            precision=lax.Precision.HIGHEST, preferred_element_type=f32,
        )

        def sent(slot, carry):
            small_copy(step, slot, small_own).wait_send()

            def scale_sent():
                scale_copy(step, slot, far(slot)).wait_send()

            if relayed:
                pl.when(slot != 1)(scale_sent)
            else:
                scale_sent()

            def sent_tile(tile, carry):
                base_copy(step, slot, tile, base_own.at[rows_of(tile)]).wait_send()
                cot_copy(step, slot, far(slot), tile).wait_send()
                return carry

            return lax.fori_loop(0, tiles, sent_tile, carry)

        lax.fori_loop(0, 4, sent, 0)
        return carry

    lax.fori_loop(0, steps, one_step, 0)


def pick_kernel(index_ref, data_ref, out_ref, sem):
    steps, count = index_ref.shape
    copies = [
        pltpu.make_async_copy(
            data_ref.at[index_ref[i // count, i % count]], out_ref.at[i], sem.at[i]
        )
        for i in range(steps * count)
    ]
    for copy in copies:
        copy.start()
    for copy in copies:
        copy.wait()


def pick(data, index):
    count = index.size
    return pl.pallas_call(
        pick_kernel,
        out_shape=jax.ShapeDtypeStruct((count,) + data.shape[1:], data.dtype),
        in_specs=[
            pl.BlockSpec(memory_space=pltpu.SMEM), pl.BlockSpec(memory_space=pl.ANY)
        ],
        out_specs=pl.BlockSpec(memory_space=pltpu.VMEM),
        scratch_shapes=[pltpu.SemaphoreType.DMA((count,))],
        compiler_params=pltpu.CompilerParams(vmem_limit_bytes=58 * 1024 * 1024),
    )(index, data)


def on_device(
    rows_count, cols_count,
    data, real_index, latent_seed, latent_bank, g_in, g_base, g_one, g_two, d_one, d_two, d_out,
):
    steps = real_index.shape[2]
    places, channels = data.shape[3:]
    reals = pick(data[0, 0], real_index[0, 0])
    wide = 2 * channels
    square = (channels, channels)
    blocks = pltpu.VMEM((wide, wide), bf16)
    tiles = places // TILE
    vmem = pl.BlockSpec(memory_space=pltpu.VMEM)
    small = 2 * channels + 16
    shapes = [square, (places, channels), square, square, square, square, (1, channels)]
    outs = pl.pallas_call(
        functools.partial(train_kernel, rows_count, cols_count, steps),
        out_shape=[jax.ShapeDtypeStruct(shape, f32) for shape in shapes]
        + [jax.ShapeDtypeStruct((steps, 6, 8, channels), f32)],
        in_specs=[vmem, pl.BlockSpec(memory_space=pltpu.SMEM)] + [vmem] * 8,
        out_specs=[vmem] * 8,
        scratch_shapes=[
            pltpu.VMEM((small, channels), bf16),
            pltpu.VMEM((places, channels), bf16),
            pltpu.VMEM((steps, 4, small, channels), bf16),
            pltpu.VMEM((steps, 4, places, channels), bf16),
            pltpu.VMEM((places, wide), bf16),
            pltpu.VMEM((steps, 4, places, wide), bf16),
            pltpu.VMEM((steps, 4, places, wide), bf16),
            pltpu.VMEM((8, wide), f32),
            pltpu.VMEM((steps, 4, 8, wide), f32),
            pltpu.VMEM((steps, 4, 8, wide), f32),
            pltpu.VMEM((places, wide), bf16),
            pltpu.VMEM((places, wide), bf16),
            pltpu.VMEM((places, wide), f32),
            pltpu.VMEM((places, wide), f32),
        ]
        + [blocks] * 10
        + [
            pltpu.VMEM((wide, wide), f32),
            pltpu.VMEM((wide, wide), f32),
            pltpu.VMEM((1, wide), f32),
            pltpu.VMEM(square, f32),
            pltpu.VMEM(square, f32),
            pltpu.VMEM((1, channels), f32),
            pltpu.VMEM((steps, 8, channels), f32),
            pltpu.SemaphoreType.DMA((steps, 4, tiles + 1)),
            pltpu.SemaphoreType.DMA((steps, 4, tiles + 1)),
            pltpu.SemaphoreType.DMA((steps, 4, tiles)),
            pltpu.SemaphoreType.DMA((steps, 4, tiles)),
            pltpu.SemaphoreType.DMA((steps, 4)),
            pltpu.SemaphoreType.DMA((steps, 4)),
        ],
        compiler_params=pltpu.CompilerParams(
            collective_id=0, has_side_effects=True, vmem_limit_bytes=50 * 1024 * 1024
        ),
    )(
        reals, latent_seed[0, 0], latent_bank,
        g_in[0, 0], g_base[0, 0], g_one[0, 0], g_two[0, 0], d_one[0, 0], d_two[0, 0],
        d_out.reshape(1, channels),
    )
    verdicts = outs[7][:, :, :2, 0].reshape(1, 1, steps, 12)
    finals = [member[None, None] for member in outs[:6]] + [outs[6].reshape(1, 1, channels)]
    return (*finals, verdicts)


def solution(mesh):
    whole = P("row", "col", None, None)
    return jax.shard_map(
        functools.partial(on_device, mesh.shape["row"], mesh.shape["col"]),
        mesh=mesh,
        in_specs=(P("row", "col", None, None, None), whole, whole, P()) + (whole,) * 6
        + (P("row", "col", None),),
        out_specs=(whole,) * 6 + (P("row", "col", None), whole),
        check_vma=False,
    )
```
